512 devices in a mesh: loop: 32 (over z_hi, x, y), grp: 16 (over z_lo, core).
Axes of the slice: x: 4, y: 4, z: 16 (z_hi: 2, z_lo: 8; z = z_hi * 8 + z_lo), core: 2. Of those that a mesh axis runs over, the one named last changes fastest.
Arguments:
- views: bfloat16 [8192, 1024], P(('loop', 'grp')), may hold values from -2 to 2
- partner: int32 [8192], P(('loop', 'grp')), may hold values from 0 to 8191, as said below
Outputs:
- view_loss: float32 [8192], P(('loop', 'grp'))
- derivative_samples: bfloat16 [8192, 1024], P(('loop', 'grp'))
The draws below stay inside these ranges and needn't reach their ends.
Inputs may be any that keep to these rules, and one draw needn't show every extreme that they name: partner pairs the views: partner[partner[i]] == i and partner[i] != i.
All inputs are finite; a program needn't handle non-finite values.
Results may differ from the reference program's by a relative error of at most 0.0085.
Values may be sent and summed in bfloat16 or wider, within the bound.
No kernel may reach another device: no remote copies, remote signals or barrier semaphores. Data moves between devices by JAX's collectives and lax.ppermute only.
A program may use at most 64 MiB of HBM per device.

```python
import jax
import jax.numpy as jnp
from jax import lax

FEATURE_WIDTH = 1024
V_DEV = 16
SAMPLE_TOTAL = 8192
N_LOOP = 32
N_GRP = 16


def draw_views(key, part):
    key = jax.random.fold_in(key, 1)
    values = jax.random.normal(key, (SAMPLE_TOTAL, FEATURE_WIDTH), jnp.float32) * 0.1
    return jnp.clip(values, -0.6, 0.6).astype(jnp.bfloat16)


def draw_partner(key, part):
    key = jax.random.fold_in(key, 2)
    order = jax.random.permutation(key, SAMPLE_TOTAL).astype(jnp.int32)
    slots = jnp.arange(SAMPLE_TOTAL, dtype=jnp.int32)
    mates = order[jnp.bitwise_xor(slots, 1)]
    return jnp.zeros((SAMPLE_TOTAL,), jnp.int32).at[order].set(mates)


def setup_inputs(seed: int = 0) -> dict:
    splits = jax.random.split(jax.random.key(seed), 3)
    views = draw_views(jax.random.fold_in(splits[2], 71), 0)
    partner = draw_partner(jax.random.fold_in(splits[2], 71), 0)
    return {"views": views, "partner": partner}


def reference(views, partner):
    group_rows = V_DEV * N_GRP
    all_ids = jnp.arange(SAMPLE_TOTAL, dtype=jnp.int32)

    def iteration_body(carry, group):
        start = (group * group_rows).astype(jnp.int32)
        rows = lax.dynamic_slice_in_dim(views, start, group_rows, 0)
        row_partner = lax.dynamic_slice_in_dim(partner, start, group_rows, 0)
        row_ids = start + jnp.arange(group_rows, dtype=jnp.int32)
        cosine_logits = 10.0 * jnp.dot(rows, views.T, preferred_element_type=jnp.float32)
        self_mask = row_ids[:, None] == all_ids[None, :]
        positive = all_ids[None, :] == row_partner[:, None]
        masked = jnp.where(self_mask, -1e30, cosine_logits)
        maxima = jnp.max(masked, axis=1)
        totals = jnp.sum(jnp.where(self_mask, 0.0, jnp.exp(masked - maxima[:, None])), axis=1)
        lse = maxima + jnp.log(totals)
        loss = lse - jnp.sum(jnp.where(positive, cosine_logits, 0.0), axis=1)
        probs = jnp.where(self_mask, 0.0, jnp.exp(masked - lse[:, None]))
        weight_matrix = (probs - positive.astype(jnp.float32)).astype(jnp.bfloat16)
        left_multiplier = 10.0 * jnp.dot(weight_matrix, views, preferred_element_type=jnp.float32)
        column = 10.0 * lax.dot_general(weight_matrix, rows, (((0,), (0,)), ((), ())), preferred_element_type=jnp.float32)
        return carry + column, (loss, left_multiplier)

    vertical_total_pooled, (objective_entries, former_summand_parts) = lax.scan(iteration_body, jnp.zeros((SAMPLE_TOTAL, FEATURE_WIDTH), jnp.float32), jnp.arange(N_LOOP, dtype=jnp.int32))
    derivative_samples = (former_summand_parts.reshape(SAMPLE_TOTAL, FEATURE_WIDTH) + vertical_total_pooled).astype(jnp.bfloat16)
    return objective_entries.reshape(SAMPLE_TOTAL), derivative_samples
```

```python
import jax
import jax.numpy as jnp
from jax import lax
from jax.sharding import Mesh, PartitionSpec as P

inverse_softness = 10.0
very_low = -1e30
shard = 16

NAMES = ("zh", "x", "y", "zl", "core")
PLANE = ("x", "y")
LINE = ("zh", "zl")


def local(views, partner):
    zh, x, y, zl, core = (lax.axis_index(n) for n in NAMES)
    width = views.shape[1]
    digits = jnp.stack([partner // 128, partner % 128], axis=1).astype(jnp.bfloat16)
    packed = jnp.concatenate([views, jnp.pad(digits, ((0, 0), (0, 126)))], axis=1)
    spread = jnp.broadcast_to(packed[None], (16, shard, width + 128))
    rows = lax.all_to_all(spread, PLANE, 0, 0)
    row_views = rows[:, :, :width].reshape(256, width)
    rows_partner = (
        rows[:, :, width].astype(jnp.int32) * 128 + rows[:, :, width + 1].astype(jnp.int32)
    ).reshape(256)
    line = lax.all_gather(views, LINE, axis=0, tiled=True)
    column_views = lax.all_gather(line, "core", axis=0, tiled=True)

    r = jnp.arange(256, dtype=jnp.int32)
    row_ids = ((zh * 16 + r // 16) * 16 + zl * 2 + core) * 16 + r % 16
    c = jnp.arange(512, dtype=jnp.int32)
    column_ids = ((c // 128 % 2 * 16 + x * 4 + y) * 16 + c // 16 % 8 * 2 + c // 256) * 16 + c % 16

    scores = inverse_softness * jnp.dot(
        row_views, column_views.T, preferred_element_type=jnp.float32
    )
    positive = column_ids[None, :] == rows_partner[:, None]
    masked = jnp.where(row_ids[:, None] == column_ids[None, :], very_low, scores)
    picked = jnp.sum(jnp.where(positive, scores, 0.0), axis=1)
    row_top = jnp.max(masked, axis=1)
    row_part = row_top + jnp.log(jnp.sum(jnp.exp(masked - row_top[:, None]), axis=1))
    column_top = jnp.max(masked, axis=0)
    column_part = column_top + jnp.log(jnp.sum(jnp.exp(masked - column_top[None, :]), axis=0))

    row_stats = lax.all_to_all(
        jnp.broadcast_to(jnp.stack([row_part, picked])[None], (16, 2, 256)), PLANE, 0, 0
    )
    column_stats = lax.all_to_all(
        jnp.broadcast_to(column_part.reshape(1, 4, 128), (32, 4, 128)), LINE + ("core",), 0, 0
    ).reshape(32, 512)
    row_lse = jax.nn.logsumexp(row_stats[:, 0], axis=0)
    column_lse = jax.nn.logsumexp(column_stats, axis=0)
    loss = row_lse - jnp.sum(row_stats[:, 1], axis=0)
    view_loss = lax.dynamic_slice_in_dim(loss, (x * 4 + y) * shard, shard, 0)

    weight = (
        jnp.exp(masked - row_lse[:, None])
        + jnp.exp(masked - column_lse[None, :])
        - 2.0 * positive.astype(jnp.float32)
    ).astype(jnp.bfloat16)
    term = inverse_softness * jnp.dot(weight, column_views, preferred_element_type=jnp.float32)
    parts = lax.all_to_all(term.astype(jnp.bfloat16).reshape(16, shard, width), PLANE, 0, 0)
    derivative = jnp.sum(parts.astype(jnp.float32), axis=0).astype(jnp.bfloat16)
    return view_loss, derivative


def solution(mesh):
    split = Mesh(mesh.devices.reshape(2, 4, 4, 8, 2), NAMES)
    in_specs = (P(NAMES, None), P(NAMES))
    out_specs = (P(NAMES), P(NAMES, None))
    return jax.shard_map(
        local, mesh=split, in_specs=in_specs, out_specs=out_specs, check_vma=False
    )
```

```python
import jax
import jax.numpy as jnp
from jax import lax
from jax.sharding import Mesh, PartitionSpec as P

inverse_softness = 10.0
very_low = -1e30
shard = 16

NAMES = ("zh", "x", "y", "zl", "core")
PLANE = ("x", "y")
LINE = ("zh", "zl")


def local(views, partner):
    zh, x, y, zl, core = (lax.axis_index(n) for n in NAMES)
    width = views.shape[1]
    digits = jnp.stack([partner // 128, partner % 128], axis=1).astype(jnp.bfloat16)
    packed = jnp.concatenate([views, jnp.pad(digits, ((0, 0), (0, 126)))], axis=1)
    line = lax.all_to_all(jnp.broadcast_to(views[None], (16, shard, width)), LINE, 0, 0)
    rows = lax.all_gather(packed, PLANE, axis=0, tiled=True)
    line, rows = lax.optimization_barrier((line.reshape(256, width), rows))
    row_views = rows[:, :width]
    rows_partner = rows[:, width].astype(jnp.int32) * 128 + rows[:, width + 1].astype(jnp.int32)
    other = lax.ppermute(line, "core", [(0, 1), (1, 0)])
    column_views = jnp.concatenate([line, other])

    def swap(per_column):
        return jnp.where(core == 0, per_column, jnp.roll(per_column, 256))

    r = jnp.arange(256, dtype=jnp.int32)
    row_ids = ((zh * 16 + r // 16) * 16 + zl * 2 + core) * 16 + r % 16
    c = jnp.arange(512, dtype=jnp.int32)
    column_ids = ((c // 128 % 2 * 16 + x * 4 + y) * 16 + c // 16 % 8 * 2 + (core ^ (c // 256))) * 16 + c % 16

    scores = inverse_softness * jnp.dot(
        row_views, column_views.T, preferred_element_type=jnp.float32
    )
    positive = column_ids[None, :] == rows_partner[:, None]
    masked = jnp.where(row_ids[:, None] == column_ids[None, :], very_low, scores)
    picked = jnp.sum(jnp.where(positive, scores, 0.0), axis=1)
    row_top = jnp.max(masked, axis=1)
    row_part = row_top + jnp.log(jnp.sum(jnp.exp(masked - row_top[:, None]), axis=1))
    column_top = jnp.max(masked, axis=0)
    column_part = column_top + jnp.log(jnp.sum(jnp.exp(masked - column_top[None, :]), axis=0))

    row_stats = lax.all_to_all(
        jnp.broadcast_to(jnp.stack([row_part, picked])[None], (16, 2, 256)), PLANE, 0, 0
    )
    column_stats = lax.all_to_all(
        jnp.broadcast_to(swap(column_part).reshape(1, 4, 128), (32, 4, 128)), LINE + ("core",), 0, 0
    ).reshape(32, 512)
    row_lse = jax.nn.logsumexp(row_stats[:, 0], axis=0)
    column_lse = swap(jax.nn.logsumexp(column_stats, axis=0))
    loss = row_lse - jnp.sum(row_stats[:, 1], axis=0)
    view_loss = lax.dynamic_slice_in_dim(loss, (x * 4 + y) * shard, shard, 0)

    weight = (
        jnp.exp(masked - row_lse[:, None])
        + jnp.exp(masked - column_lse[None, :])
        - 2.0 * positive.astype(jnp.float32)
    ).astype(jnp.bfloat16)
    term = inverse_softness * jnp.dot(weight, column_views, preferred_element_type=jnp.float32)
    parts = lax.all_to_all(term.astype(jnp.bfloat16).reshape(16, shard, width), PLANE, 0, 0)
    derivative = jnp.sum(parts.astype(jnp.float32), axis=0).astype(jnp.bfloat16)
    return view_loss, derivative


def solution(mesh):
    split = Mesh(mesh.devices.reshape(2, 4, 4, 8, 2), NAMES)
    in_specs = (P(NAMES, None), P(NAMES))
    out_specs = (P(NAMES), P(NAMES, None))
    return jax.shard_map(
        local, mesh=split, in_specs=in_specs, out_specs=out_specs, check_vma=False
    )
```

```python
import jax
import jax.numpy as jnp
from jax import lax
from jax.sharding import Mesh, PartitionSpec as P

inverse_softness = 10.0
very_low = -1e30
shard = 16

NAMES = ("zh", "x", "y", "zl", "core")
PLANE = ("x", "y")
LINE = ("zh", "zl")


def local(views, partner):
    zh, x, y, zl, core = (lax.axis_index(n) for n in NAMES)
    width = views.shape[1]
    digits = jnp.stack([partner // 128, partner % 128], axis=1).astype(jnp.bfloat16)
    packed = jnp.concatenate([views, jnp.pad(digits, ((0, 0), (0, 126)))], axis=1)
    line = lax.all_to_all(jnp.broadcast_to(views[None], (16, shard, width)), LINE, 0, 0)
    rows = lax.all_gather(packed, PLANE, axis=0, tiled=True)
    line, rows = lax.optimization_barrier((line.reshape(256, width), rows))
    row_views = rows[:, :width]
    rows_partner = rows[:, width].astype(jnp.int32) * 128 + rows[:, width + 1].astype(jnp.int32)
    other = lax.ppermute(line, "core", [(0, 1), (1, 0)])
    column_views = jnp.concatenate([line, other])

    def swap(per_column):
        return jnp.where(core == 0, per_column, jnp.roll(per_column, 256))

    r = jnp.arange(256, dtype=jnp.int32)
    row_ids = ((zh * 16 + r // 16) * 16 + zl * 2 + core) * 16 + r % 16
    c = jnp.arange(512, dtype=jnp.int32)
    column_ids = ((c // 128 % 2 * 16 + x * 4 + y) * 16 + c // 16 % 8 * 2 + (core ^ (c // 256))) * 16 + c % 16

    scores = inverse_softness * jnp.dot(
        row_views, column_views.T, preferred_element_type=jnp.float32
    )
    positive = column_ids[None, :] == rows_partner[:, None]
    masked = jnp.where(row_ids[:, None] == column_ids[None, :], very_low, scores)
    picked = jnp.sum(jnp.where(positive, scores, 0.0), axis=1)
    row_top = jnp.max(masked, axis=1)
    row_part = row_top + jnp.log(jnp.sum(jnp.exp(masked - row_top[:, None]), axis=1))
    column_top = jnp.max(masked, axis=0)
    column_part = column_top + jnp.log(jnp.sum(jnp.exp(masked - column_top[None, :]), axis=0))

    row_out = jnp.broadcast_to(jnp.stack([row_part, picked])[None], (16, 2, 256))
    column_out = jnp.broadcast_to(swap(column_part).reshape(1, 4, 128), (32, 4, 128))
    row_out, column_out = lax.optimization_barrier((row_out, column_out))
    row_stats = lax.all_gather(row_out[0], PLANE)
    column_stats = lax.all_to_all(column_out, LINE + ("core",), 0, 0)
    row_stats, column_stats = lax.optimization_barrier((row_stats, column_stats))
    column_stats = column_stats.reshape(32, 512)
    row_lse = jax.nn.logsumexp(row_stats[:, 0], axis=0)
    column_lse = swap(jax.nn.logsumexp(column_stats, axis=0))
    loss = row_lse - jnp.sum(row_stats[:, 1], axis=0)
    view_loss = lax.dynamic_slice_in_dim(loss, (x * 4 + y) * shard, shard, 0)

    weight = (
        jnp.exp(masked - row_lse[:, None])
        + jnp.exp(masked - column_lse[None, :])
        - 2.0 * positive.astype(jnp.float32)
    ).astype(jnp.bfloat16)
    term = inverse_softness * jnp.dot(weight, column_views, preferred_element_type=jnp.float32)
    parts = lax.all_to_all(term.astype(jnp.bfloat16).reshape(16, shard, width), PLANE, 0, 0)
    derivative = jnp.sum(parts.astype(jnp.float32), axis=0).astype(jnp.bfloat16)
    return view_loss, derivative


def solution(mesh):
    split = Mesh(mesh.devices.reshape(2, 4, 4, 8, 2), NAMES)
    in_specs = (P(NAMES, None), P(NAMES))
    out_specs = (P(NAMES), P(NAMES, None))
    return jax.shard_map(
        local, mesh=split, in_specs=in_specs, out_specs=out_specs, check_vma=False
    )
```

```python
import jax
import jax.numpy as jnp
from jax import lax
from jax.sharding import Mesh, PartitionSpec as P

inverse_softness = 10.0
very_low = -1e30
shard = 16

NAMES = ("zh", "x", "y", "zl", "core")
PLANE = ("x", "y")
LINE = ("zh", "zl")


def combine(stats):
    return jnp.stack([jax.nn.logsumexp(stats[:, 0], axis=0), jnp.sum(stats[:, 1], axis=0)])


def local(views, partner):
    zh, x, y, zl, core = (lax.axis_index(n) for n in NAMES)
    width = views.shape[1]
    digits = jnp.stack([partner // 128, partner % 128], axis=1).astype(jnp.bfloat16)
    packed = jnp.concatenate([views, jnp.pad(digits, ((0, 0), (0, 126)))], axis=1)
    line = lax.all_to_all(jnp.broadcast_to(views[None], (16, shard, width)), LINE, 0, 0)
    rows = lax.all_gather(packed, PLANE, axis=0, tiled=True)
    line, rows = lax.optimization_barrier((line.reshape(256, width), rows))
    row_views = rows[:, :width]
    rows_partner = rows[:, width].astype(jnp.int32) * 128 + rows[:, width + 1].astype(jnp.int32)
    other = lax.ppermute(line, "core", [(0, 1), (1, 0)])
    column_views = jnp.concatenate([line, other])

    def swap(per_column):
        return jnp.where(core == 0, per_column, jnp.roll(per_column, 256))

    r = jnp.arange(256, dtype=jnp.int32)
    row_ids = ((zh * 16 + r // 16) * 16 + zl * 2 + core) * 16 + r % 16
    c = jnp.arange(512, dtype=jnp.int32)
    column_ids = ((c // 128 % 2 * 16 + x * 4 + y) * 16 + c // 16 % 8 * 2 + (core ^ (c // 256))) * 16 + c % 16

    scores = inverse_softness * jnp.dot(
        row_views, column_views.T, preferred_element_type=jnp.float32
    )
    positive = column_ids[None, :] == rows_partner[:, None]
    masked = jnp.where(row_ids[:, None] == column_ids[None, :], very_low, scores)
    picked = jnp.sum(jnp.where(positive, scores, 0.0), axis=1)
    row_top = jnp.max(masked, axis=1)
    row_part = row_top + jnp.log(jnp.sum(jnp.exp(masked - row_top[:, None]), axis=1))
    column_top = jnp.max(masked, axis=0)
    column_part = column_top + jnp.log(jnp.sum(jnp.exp(masked - column_top[None, :]), axis=0))

    column_out = jnp.broadcast_to(swap(column_part).reshape(1, 4, 128), (32, 4, 128))
    row_stats = jnp.stack([row_part, picked])
    column_stats = lax.all_to_all(column_out, LINE + ("core",), 0, 0)
    row_stats = combine(lax.all_gather(row_stats, "x"))
    row_stats = lax.all_gather(row_stats, "y")
    row_stats, column_stats = lax.optimization_barrier((row_stats, column_stats))
    row_lse, picked = combine(row_stats)
    column_lse = swap(jax.nn.logsumexp(column_stats.reshape(32, 512), axis=0))
    loss = row_lse - picked
    view_loss = lax.dynamic_slice_in_dim(loss, (x * 4 + y) * shard, shard, 0)

    weight = (
        jnp.exp(masked - row_lse[:, None])
        + jnp.exp(masked - column_lse[None, :])
        - 2.0 * positive.astype(jnp.float32)
    ).astype(jnp.bfloat16)
    term = inverse_softness * jnp.dot(weight, column_views, preferred_element_type=jnp.float32)
    parts = lax.all_to_all(term.astype(jnp.bfloat16).reshape(16, shard, width), PLANE, 0, 0)
    derivative = jnp.sum(parts.astype(jnp.float32), axis=0).astype(jnp.bfloat16)
    return view_loss, derivative


def solution(mesh):
    split = Mesh(mesh.devices.reshape(2, 4, 4, 8, 2), NAMES)
    in_specs = (P(NAMES, None), P(NAMES))
    out_specs = (P(NAMES), P(NAMES, None))
    return jax.shard_map(
        local, mesh=split, in_specs=in_specs, out_specs=out_specs, check_vma=False
    )
```

```python
import jax
import jax.numpy as jnp
from jax import lax
from jax.sharding import Mesh, PartitionSpec as P

inverse_softness = 10.0
very_low = -1e30
shard = 16

NAMES = ("zh", "x", "y", "zl", "core")
PLANE = ("x", "y")
LINE = ("zh", "zl")


def combine(stats):
    return jnp.stack([jax.nn.logsumexp(stats[:, 0], axis=0), jnp.sum(stats[:, 1], axis=0)])


def slots(stats, axis):
    n = lax.axis_size(axis)
    mine = jnp.arange(n)[:, None, None] == lax.axis_index(axis)
    return lax.psum(jnp.where(mine, stats[None], 0.0), axis)


def local(views, partner):
    zh, x, y, zl, core = (lax.axis_index(n) for n in NAMES)
    width = views.shape[1]
    digits = jnp.stack([partner // 128, partner % 128], axis=1).astype(jnp.bfloat16)
    packed = jnp.concatenate([views, jnp.pad(digits, ((0, 0), (0, 126)))], axis=1)
    line = lax.all_to_all(jnp.broadcast_to(views[None], (16, shard, width)), LINE, 0, 0)
    rows = lax.all_gather(packed, PLANE, axis=0, tiled=True)
    line, rows = lax.optimization_barrier((line.reshape(256, width), rows))
    row_views = rows[:, :width]
    rows_partner = rows[:, width].astype(jnp.int32) * 128 + rows[:, width + 1].astype(jnp.int32)
    other = lax.ppermute(line, "core", [(0, 1), (1, 0)])
    column_views = jnp.concatenate([line, other])

    def swap(per_column):
        return jnp.where(core == 0, per_column, jnp.roll(per_column, 256))

    r = jnp.arange(256, dtype=jnp.int32)
    row_ids = ((zh * 16 + r // 16) * 16 + zl * 2 + core) * 16 + r % 16
    c = jnp.arange(512, dtype=jnp.int32)
    column_ids = ((c // 128 % 2 * 16 + x * 4 + y) * 16 + c // 16 % 8 * 2 + (core ^ (c // 256))) * 16 + c % 16

    scores = inverse_softness * jnp.dot(
        row_views, column_views.T, preferred_element_type=jnp.float32
    )
    positive = column_ids[None, :] == rows_partner[:, None]
    masked = jnp.where(row_ids[:, None] == column_ids[None, :], very_low, scores)
    picked = jnp.sum(jnp.where(positive, scores, 0.0), axis=1)
    row_top = jnp.max(masked, axis=1)
    row_part = row_top + jnp.log(jnp.sum(jnp.exp(masked - row_top[:, None]), axis=1))
    column_top = jnp.max(masked, axis=0)
    column_part = column_top + jnp.log(jnp.sum(jnp.exp(masked - column_top[None, :]), axis=0))

    column_out = jnp.broadcast_to(swap(column_part).reshape(1, 4, 128), (32, 4, 128))
    row_stats = jnp.stack([row_part, picked])
    column_stats = lax.all_to_all(column_out, LINE + ("core",), 0, 0)
    row_stats = combine(slots(row_stats, "x"))
    row_stats = slots(row_stats, "y")
    row_stats, column_stats = lax.optimization_barrier((row_stats, column_stats))
    row_lse, picked = combine(row_stats)
    column_lse = swap(jax.nn.logsumexp(column_stats.reshape(32, 512), axis=0))
    loss = row_lse - picked
    view_loss = lax.dynamic_slice_in_dim(loss, (x * 4 + y) * shard, shard, 0)

    weight = (
        jnp.exp(masked - row_lse[:, None])
        + jnp.exp(masked - column_lse[None, :])
        - 2.0 * positive.astype(jnp.float32)
    ).astype(jnp.bfloat16)
    term = inverse_softness * jnp.dot(weight, column_views, preferred_element_type=jnp.float32)
    parts = lax.all_to_all(term.astype(jnp.bfloat16).reshape(16, shard, width), PLANE, 0, 0)
    derivative = jnp.sum(parts.astype(jnp.float32), axis=0).astype(jnp.bfloat16)
    return view_loss, derivative


def solution(mesh):
    split = Mesh(mesh.devices.reshape(2, 4, 4, 8, 2), NAMES)
    in_specs = (P(NAMES, None), P(NAMES))
    out_specs = (P(NAMES), P(NAMES, None))
    return jax.shard_map(
        local, mesh=split, in_specs=in_specs, out_specs=out_specs, check_vma=False
    )
```

```python
import jax
import jax.numpy as jnp
from jax import lax
from jax.sharding import Mesh, PartitionSpec as P

inverse_softness = 10.0
very_low = -1e30
shard = 16

NAMES = ("zh", "x", "y", "zl", "core")
PLANE = ("x", "y")
LINE = ("zh", "zl")
FIRST = 13
ORDER = [[(FIRST + i) % 16 for i in range(16)]]


def combine(stats):
    return jnp.stack([jax.nn.logsumexp(stats[:, 0], axis=0), jnp.sum(stats[:, 1], axis=0)])


def slots(stats, axis):
    n = lax.axis_size(axis)
    mine = jnp.arange(n)[:, None, None] == lax.axis_index(axis)
    return lax.psum(jnp.where(mine, stats[None], 0.0), axis)


def local(views, partner):
    zh, x, y, zl, core = (lax.axis_index(n) for n in NAMES)
    width = views.shape[1]
    digits = jnp.stack([partner // 128, partner % 128], axis=1).astype(jnp.bfloat16)
    packed = jnp.concatenate([views, jnp.pad(digits, ((0, 0), (0, 126)))], axis=1)
    line = lax.all_to_all(
        jnp.broadcast_to(views[None], (16, shard, width)), LINE, 0, 0, axis_index_groups=ORDER
    )
    rows = lax.all_gather(packed, PLANE, axis=0, tiled=True)
    line, rows = lax.optimization_barrier((line.reshape(256, width), rows))
    row_views = rows[:, :width]
    rows_partner = rows[:, width].astype(jnp.int32) * 128 + rows[:, width + 1].astype(jnp.int32)
    other = lax.ppermute(line, "core", [(0, 1), (1, 0)])
    column_views = jnp.concatenate([line, other])

    def swap(per_column):
        return jnp.where(core == 0, per_column, jnp.roll(per_column, 256))

    r = jnp.arange(256, dtype=jnp.int32)
    row_ids = ((zh * 16 + r // 16) * 16 + zl * 2 + core) * 16 + r % 16
    c = jnp.arange(512, dtype=jnp.int32)
    z = (c // 16 + FIRST) % 16
    column_ids = ((z // 8 * 16 + x * 4 + y) * 16 + z % 8 * 2 + (core ^ (c // 256))) * 16 + c % 16

    scores = inverse_softness * jnp.dot(
        row_views, column_views.T, preferred_element_type=jnp.float32
    )
    positive = column_ids[None, :] == rows_partner[:, None]
    masked = jnp.where(row_ids[:, None] == column_ids[None, :], very_low, scores)
    picked = jnp.sum(jnp.where(positive, scores, 0.0), axis=1)
    row_top = jnp.max(masked, axis=1)
    row_part = row_top + jnp.log(jnp.sum(jnp.exp(masked - row_top[:, None]), axis=1))
    column_top = jnp.max(masked, axis=0)
    column_part = column_top + jnp.log(jnp.sum(jnp.exp(masked - column_top[None, :]), axis=0))

    column_out = jnp.broadcast_to(swap(column_part).reshape(1, 4, 128), (32, 4, 128))
    row_stats = jnp.stack([row_part, picked])
    column_stats = lax.all_to_all(column_out, LINE + ("core",), 0, 0)
    row_stats = combine(slots(row_stats, "x"))
    row_stats = slots(row_stats, "y")
    row_stats, column_stats = lax.optimization_barrier((row_stats, column_stats))
    row_lse, picked = combine(row_stats)
    column_lse = swap(jax.nn.logsumexp(column_stats.reshape(32, 512), axis=0))
    loss = row_lse - picked
    view_loss = lax.dynamic_slice_in_dim(loss, (x * 4 + y) * shard, shard, 0)

    weight = (
        jnp.exp(masked - row_lse[:, None])
        + jnp.exp(masked - column_lse[None, :])
        - 2.0 * positive.astype(jnp.float32)
    ).astype(jnp.bfloat16)
    term = inverse_softness * jnp.dot(weight, column_views, preferred_element_type=jnp.float32)
    parts = lax.all_to_all(term.astype(jnp.bfloat16).reshape(16, shard, width), PLANE, 0, 0)
    derivative = jnp.sum(parts.astype(jnp.float32), axis=0).astype(jnp.bfloat16)
    return view_loss, derivative


def solution(mesh):
    split = Mesh(mesh.devices.reshape(2, 4, 4, 8, 2), NAMES)
    in_specs = (P(NAMES, None), P(NAMES))
    out_specs = (P(NAMES), P(NAMES, None))
    return jax.shard_map(
        local, mesh=split, in_specs=in_specs, out_specs=out_specs, check_vma=False
    )
```

```python
import jax
import jax.numpy as jnp
from jax import lax
from jax.sharding import Mesh, PartitionSpec as P

inverse_softness = 10.0
very_low = -1e30
shard = 16

NAMES = ("zh", "x", "y", "zl", "core")
PLANE = ("x", "y")
LINE = ("zh", "zl")
FIRST = 13
ORDER = [[(FIRST + i) % 16 for i in range(16)]]


def slots(stats, axis):
    n = lax.axis_size(axis)
    mine = jnp.arange(n)[:, None] == lax.axis_index(axis)
    return lax.psum(jnp.where(mine, stats[None], 0.0), axis)


def local(views, partner):
    zh, x, y, zl, core = (lax.axis_index(n) for n in NAMES)
    width = views.shape[1]
    digits = jnp.stack([partner // 128, partner % 128], axis=1).astype(jnp.bfloat16)
    packed = jnp.concatenate([views, jnp.pad(digits, ((0, 0), (0, 126)))], axis=1)
    line = lax.all_to_all(
        jnp.broadcast_to(views[None], (16, shard, width)), LINE, 0, 0, axis_index_groups=ORDER
    )
    rows = lax.all_gather(packed, PLANE, axis=0, tiled=True)
    line, rows = lax.optimization_barrier((line.reshape(256, width), rows))
    row_views = rows[:, :width]
    rows_partner = rows[:, width].astype(jnp.int32) * 128 + rows[:, width + 1].astype(jnp.int32)
    other = lax.ppermute(line, "core", [(0, 1), (1, 0)])
    column_views = jnp.concatenate([line, other])

    def swap(per_column):
        return jnp.where(core == 0, per_column, jnp.roll(per_column, 256))

    r = jnp.arange(256, dtype=jnp.int32)
    row_ids = ((zh * 16 + r // 16) * 16 + zl * 2 + core) * 16 + r % 16
    c = jnp.arange(512, dtype=jnp.int32)
    z = (c // 16 + FIRST) % 16
    column_ids = ((z // 8 * 16 + x * 4 + y) * 16 + z % 8 * 2 + (core ^ (c // 256))) * 16 + c % 16

    scores = inverse_softness * jnp.dot(
        row_views, column_views.T, preferred_element_type=jnp.float32
    )
    positive = column_ids[None, :] == rows_partner[:, None]
    masked = jnp.where(row_ids[:, None] == column_ids[None, :], very_low, scores)
    picked = jnp.sum(jnp.where(positive, scores, 0.0), axis=0)
    row_top = jnp.max(masked, axis=1)
    row_part = row_top + jnp.log(jnp.sum(jnp.exp(masked - row_top[:, None]), axis=1))
    column_top = jnp.max(masked, axis=0)
    column_part = column_top + jnp.log(jnp.sum(jnp.exp(masked - column_top[None, :]), axis=0))

    column_out = jnp.stack([swap(column_part), swap(picked)]).reshape(1, 8, 128)
    column_out = jnp.broadcast_to(column_out, (32, 8, 128))
    column_stats = lax.all_to_all(column_out, LINE + ("core",), 0, 0)
    row_part = jax.nn.logsumexp(slots(row_part, "x"), axis=0)
    row_stats = slots(row_part, "y")
    row_stats, column_stats = lax.optimization_barrier((row_stats, column_stats))
    row_lse = jax.nn.logsumexp(row_stats, axis=0)
    column_stats = column_stats.reshape(32, 2, 512)
    column_lse = swap(jax.nn.logsumexp(column_stats[:, 0], axis=0))
    loss = column_lse - swap(jnp.sum(column_stats[:, 1], axis=0))
    here = (zh * 8 + zl - FIRST) % 16
    view_loss = lax.dynamic_slice_in_dim(loss, here * shard, shard, 0)

    weight = (
        jnp.exp(masked - row_lse[:, None])
        + jnp.exp(masked - column_lse[None, :])
        - 2.0 * positive.astype(jnp.float32)
    ).astype(jnp.bfloat16)
    term = inverse_softness * jnp.dot(weight, column_views, preferred_element_type=jnp.float32)
    parts = lax.all_to_all(term.astype(jnp.bfloat16).reshape(16, shard, width), PLANE, 0, 0)
    derivative = jnp.sum(parts.astype(jnp.float32), axis=0).astype(jnp.bfloat16)
    return view_loss, derivative


def solution(mesh):
    split = Mesh(mesh.devices.reshape(2, 4, 4, 8, 2), NAMES)
    in_specs = (P(NAMES, None), P(NAMES))
    out_specs = (P(NAMES), P(NAMES, None))
    return jax.shard_map(
        local, mesh=split, in_specs=in_specs, out_specs=out_specs, check_vma=False
    )
```

```python
import jax
import jax.numpy as jnp
from jax import lax
from jax.sharding import Mesh, PartitionSpec as P

inverse_softness = 10.0
very_low = -1e30
shard = 16

NAMES = ("zh", "x", "y", "zl", "core")
PLANE = ("x", "y")
LINE = ("zh", "zl")
FIRST = 13
PAIRS = [[(4 + i) % 32 for i in range(32)]]
ORDER = [[(FIRST + i) % 16 for i in range(16)]]


def slots(stats, axis):
    n = lax.axis_size(axis)
    mine = jnp.arange(n)[:, None] == lax.axis_index(axis)
    return lax.psum(jnp.where(mine, stats[None], 0.0), axis)


def local(views, partner):
    zh, x, y, zl, core = (lax.axis_index(n) for n in NAMES)
    width = views.shape[1]
    digits = jnp.stack([partner // 128, partner % 128], axis=1).astype(jnp.bfloat16)
    packed = jnp.concatenate([views, jnp.pad(digits, ((0, 0), (0, 126)))], axis=1)
    line = lax.all_to_all(
        jnp.broadcast_to(views[None], (16, shard, width)), LINE, 0, 0, axis_index_groups=ORDER
    )
    rows = lax.all_gather(packed, PLANE, axis=0, tiled=True)
    line, rows = lax.optimization_barrier((line.reshape(256, width), rows))
    row_views = rows[:, :width]
    rows_partner = rows[:, width].astype(jnp.int32) * 128 + rows[:, width + 1].astype(jnp.int32)
    other = lax.ppermute(line, "core", [(0, 1), (1, 0)])
    column_views = jnp.concatenate([line, other])

    def swap(per_column):
        return jnp.where(core == 0, per_column, jnp.roll(per_column, 256))

    r = jnp.arange(256, dtype=jnp.int32)
    row_ids = ((zh * 16 + r // 16) * 16 + zl * 2 + core) * 16 + r % 16
    c = jnp.arange(512, dtype=jnp.int32)
    z = (c // 16 + FIRST) % 16
    column_ids = ((z // 8 * 16 + x * 4 + y) * 16 + z % 8 * 2 + (core ^ (c // 256))) * 16 + c % 16

    scores = inverse_softness * jnp.dot(
        row_views, column_views.T, preferred_element_type=jnp.float32
    )
    positive = column_ids[None, :] == rows_partner[:, None]
    masked = jnp.where(row_ids[:, None] == column_ids[None, :], very_low, scores)
    picked = jnp.sum(jnp.where(positive, scores, 0.0), axis=0)
    row_top = jnp.max(masked, axis=1)
    row_part = row_top + jnp.log(jnp.sum(jnp.exp(masked - row_top[:, None]), axis=1))
    column_top = jnp.max(masked, axis=0)
    column_part = column_top + jnp.log(jnp.sum(jnp.exp(masked - column_top[None, :]), axis=0))

    column_out = jnp.stack([swap(column_part), swap(picked)]).reshape(1, 8, 128)
    column_out = jnp.broadcast_to(column_out, (32, 8, 128))
    column_stats = lax.all_to_all(
        column_out, LINE + ("core",), 0, 0, axis_index_groups=PAIRS
    )
    row_part = jax.nn.logsumexp(slots(row_part, "x"), axis=0)
    row_stats = slots(row_part, "y")
    row_stats, column_stats = lax.optimization_barrier((row_stats, column_stats))
    row_lse = jax.nn.logsumexp(row_stats, axis=0)
    column_stats = column_stats.reshape(32, 2, 512)
    column_lse = swap(jax.nn.logsumexp(column_stats[:, 0], axis=0))
    loss = column_lse - swap(jnp.sum(column_stats[:, 1], axis=0))
    here = (zh * 8 + zl - FIRST) % 16
    view_loss = lax.dynamic_slice_in_dim(loss, here * shard, shard, 0)

    weight = (
        jnp.exp(masked - row_lse[:, None])
        + jnp.exp(masked - column_lse[None, :])
        - 2.0 * positive.astype(jnp.float32)
    ).astype(jnp.bfloat16)
    term = inverse_softness * jnp.dot(weight, column_views, preferred_element_type=jnp.float32)
    parts = lax.all_to_all(term.astype(jnp.bfloat16).reshape(16, shard, width), PLANE, 0, 0)
    derivative = jnp.sum(parts.astype(jnp.float32), axis=0).astype(jnp.bfloat16)
    return view_loss, derivative


def solution(mesh):
    split = Mesh(mesh.devices.reshape(2, 4, 4, 8, 2), NAMES)
    in_specs = (P(NAMES, None), P(NAMES))
    out_specs = (P(NAMES), P(NAMES, None))
    return jax.shard_map(
        local, mesh=split, in_specs=in_specs, out_specs=out_specs, check_vma=False
    )
```
